32 devices in a mesh: fsdp: 8 (over y, x, core), tensor: 4 (over z).
Axes of the slice: x: 2, y: 2, z: 4, core: 2. Of those that a mesh axis runs over, the one named last changes fastest.
Arguments:
- hidden_t: bfloat16 [28672, 512], P('fsdp', 'tensor'), may hold values from -6 to 6
- down_weight: bfloat16 [28672, 4096], P('fsdp', 'tensor'), may hold values from -0.03125 to 0.03125
- probe: bfloat16 [28672, 4096], P('fsdp', 'tensor'), may hold values from -5 to 5
- grad_moment: bfloat16 [28672, 4096], P('fsdp', 'tensor'), may hold values from -0.0059814453 to 0.0059814453
- curv_moment: bfloat16 [28672, 4096], P('fsdp', 'tensor'), may hold values from 0.0099487305 to 0.099609375
- target: bfloat16 [512, 4096], P('fsdp', 'tensor'), may hold values from -6 to 6
Outputs:
- new_grad_moment: bfloat16 [28672, 4096], P('fsdp', 'tensor')
- new_curv_moment: bfloat16 [28672, 4096], P('fsdp', 'tensor')
- update: bfloat16 [28672, 4096], P('fsdp', 'tensor')
The draws below stay inside these ranges and needn't reach their ends.
All inputs are finite; a program needn't handle non-finite values.
Results may differ from the reference program's by a relative error of at most 0.0056.
Values may be sent and summed in bfloat16 or wider, within the bound.
A program may use at most 192 MiB of HBM per device.

```python
import math
import jax
import jax.numpy as jnp
from jax import lax

D = 4096
FF = 28672
TOKENS = 512


def level_of(rng, dims, pieces, low, high):
    def one(dim, shards_of):
        steps = jax.random.uniform(jax.random.fold_in(jax.random.fold_in(rng, 6), dim), (shards_of,), jnp.float32, low / len(pieces), high / len(pieces))
        return jnp.repeat(jnp.exp(steps), dims[dim] // shards_of).reshape((-1,) + (1,) * (len(dims) - dim - 1))

    gain = one(*pieces[0])
    for cut in pieces[1:]:
        gain = gain * one(*cut)
    return gain


def gaussian(stream_key, shape, spread, bound, split=(), held_as=jnp.bfloat16):
    result = spread * jax.random.normal(stream_key, shape, jnp.float32)
    if split:
        result = result * level_of(stream_key, shape, split, -0.22, 0.18)
    return jnp.clip(result, -bound, bound).astype(held_as)


def setup_inputs(seed: int = 0) -> dict:
    seeds = jax.random.split(jax.random.key(seed), 7)
    return {
        "hidden_t": gaussian(seeds[0], (FF, TOKENS), 1.0, 6.0, ((0, 8), (1, 4))),
        "down_weight": gaussian(seeds[1], (FF, D), FF ** -0.5, 0.03125, ((0, 8), (1, 4))),
        "probe": gaussian(seeds[2], (FF, D), 1.0, 5.0, ((0, 8), (1, 4))),
        "grad_moment": gaussian(seeds[3], (FF, D), 0.001, 0.0059814453, ((0, 8), (1, 4))),
        "curv_moment": jnp.clip(jnp.exp(math.log(0.099609375) - 2.3038113 * jax.random.uniform(seeds[4], (FF, D), jnp.float32) ** level_of(seeds[4], (FF, D), ((0, 8), (1, 4)), -0.2, 0.2)), 0.0099487305, 0.099609375).astype(jnp.bfloat16),
        "target": gaussian(seeds[5], (TOKENS, D), 1.0, 6.0, ((0, 8), (1, 4))),
    }


BETA_ONE = 0.965
BETA_TWO = 0.99
RHO_SCALE = 0.02
EPS_FLOOR = 0.0005


def reference(hidden_t, down_weight, probe, grad_moment, curv_moment, target):
    col_width = down_weight.shape[1]
    token_count = hidden_t.shape[1]
    paired = jnp.concatenate([down_weight, probe], axis=1)
    outputs_pair = lax.dot_general(hidden_t, paired, (((0,), (0,)), ((), ())), preferred_element_type=jnp.float32)
    adjoint = ((outputs_pair[:, :col_width] - target.astype(jnp.float32)) / token_count).astype(jnp.bfloat16)
    tangent_adjoint = (outputs_pair[:, col_width:] / token_count).astype(jnp.bfloat16)
    stacked = jnp.concatenate([adjoint, tangent_adjoint], axis=1)
    products = jnp.dot(hidden_t, stacked, preferred_element_type=jnp.float32)
    gradient = products[:, :col_width]
    hess_probe = products[:, col_width:]
    estimate = probe.astype(jnp.float32) * hess_probe
    moment_next = BETA_ONE * grad_moment.astype(jnp.float32) + (1.0 - BETA_ONE) * gradient
    curv_next = BETA_TWO * curv_moment.astype(jnp.float32) + (1.0 - BETA_TWO) * estimate
    raw_ratio = moment_next / jnp.maximum(RHO_SCALE * curv_next, EPS_FLOOR)
    update = jnp.clip(raw_ratio, -1.0, 1.0)
    return moment_next.astype(jnp.bfloat16), curv_next.astype(jnp.bfloat16), update.astype(jnp.bfloat16)
```

```python
import functools

import jax
import jax.numpy as jnp
from jax import lax
from jax.experimental import pallas as pl
from jax.experimental.pallas import tpu as pltpu
from jax.sharding import PartitionSpec as P

BETA_ONE = 0.965
BETA_TWO = 0.99
RHO_SCALE = 0.02
EPS_FLOOR = 0.0005
MESH = pl.DeviceIdType.MESH
MIB = 1 << 20


def cotangents(summed, target_rows, col_width, token_count):
    adjoint = ((summed[:, :col_width] - target_rows.astype(jnp.float32)) / token_count).astype(
        jnp.bfloat16
    )
    tangent_adjoint = (summed[:, col_width:] / token_count).astype(jnp.bfloat16)
    return jnp.concatenate([adjoint, tangent_adjoint], axis=1)


def moments(products, probe, grad_moment, curv_moment):
    col_width = probe.shape[1]
    gradient = products[:, :col_width]
    hess_probe = products[:, col_width:]
    estimate = probe.astype(jnp.float32) * hess_probe
    moment_next = BETA_ONE * grad_moment.astype(jnp.float32) + (1.0 - BETA_ONE) * gradient
    curv_next = BETA_TWO * curv_moment.astype(jnp.float32) + (1.0 - BETA_TWO) * estimate
    raw_ratio = moment_next / jnp.maximum(RHO_SCALE * curv_next, EPS_FLOOR)
    update = jnp.clip(raw_ratio, -1.0, 1.0)
    return (
        moment_next.astype(jnp.bfloat16),
        curv_next.astype(jnp.bfloat16),
        update.astype(jnp.bfloat16),
    )


def plain_shards(hidden_t, down_weight, probe, grad_moment, curv_moment, target):
    gathered = lax.all_gather(hidden_t, "tensor", axis=1, tiled=True)
    col_width = down_weight.shape[1]
    token_count = gathered.shape[1]
    paired = jnp.concatenate([down_weight, probe], axis=1)
    partial_out = lax.dot_general(
        gathered, paired, (((0,), (0,)), ((), ())), preferred_element_type=jnp.float32
    )
    totals = lax.psum(partial_out, "fsdp")
    target_all = lax.all_gather(target, "fsdp", axis=0, tiled=True)
    stacked = cotangents(totals, target_all, col_width, token_count)
    products = jnp.dot(gathered, stacked, preferred_element_type=jnp.float32)
    return moments(products, probe, grad_moment, curv_moment)


def arrival_order(n_t):
    table = []
    for z in range(n_t):
        near_right = z < n_t // 2
        table.append(
            sorted(range(n_t), key=lambda b: (abs(b - z), (b < z) == near_right))
        )
    return table


def pick(values, index):
    result = jnp.int32(values[0])
    for i in range(1, len(values)):
        result = jnp.where(index == i, jnp.int32(values[i]), result)
    return result


def cotangent_kernel(
    n_f, n_t, n_c,
    hid_in, w_in, probe_in, target_in,
    gath, stk,
    wbuf, acc, part, rsbuf, tgt,
    hid_sem, w_sem, p_sem,
    left_send, right_send, gath_recv,
    rs_send, rs_recv, ag_send, ag_recv, tgt_send, tgt_recv,
):
    f = lax.axis_index("fsdp")
    z = lax.axis_index("tensor")
    rows, block_tokens = hid_in.shape
    cols = w_in.shape[1]
    chunk = rows // n_c
    piece = block_tokens // n_f
    tokens = block_tokens * n_t
    order = arrival_order(n_t)

    def cut(c):
        return pl.ds(pl.multiple_of(c * chunk, chunk), chunk)

    def span(j):
        return pl.ds(pl.multiple_of(j * piece, piece), piece)

    def hid_load(c):
        return pltpu.make_async_copy(
            hid_in.at[cut(c)], gath.at[z, cut(c)], hid_sem.at[c]
        )

    def w_load(c):
        return pltpu.make_async_copy(
            w_in.at[cut(c)], wbuf.at[cut(c), pl.ds(0, cols)], w_sem.at[c]
        )

    def p_load(c):
        return pltpu.make_async_copy(
            probe_in.at[cut(c)], wbuf.at[cut(c), pl.ds(cols, cols)], p_sem.at[c]
        )

    def pass_on(src, b, c, side):
        sems = left_send if side < 0 else right_send
        return pltpu.make_async_remote_copy(
            src_ref=src.at[cut(c)],
            dst_ref=gath.at[b, cut(c)],
            send_sem=sems.at[b, c],
            recv_sem=gath_recv.at[b, c],
            device_id=(f, z + side),
            device_id_type=MESH,
        )

    def rs_copy(b, peer, slot):
        return pltpu.make_async_remote_copy(
            src_ref=part.at[b, span(peer)],
            dst_ref=rsbuf.at[b, slot],
            send_sem=rs_send.at[b, peer],
            recv_sem=rs_recv.at[b, slot],
            device_id=(peer, z),
            device_id_type=MESH,
        )

    def ag_copy(b, peer, slot):
        return pltpu.make_async_remote_copy(
            src_ref=stk.at[b, span(slot)],
            dst_ref=stk.at[b, span(slot)],
            send_sem=ag_send.at[b, peer],
            recv_sem=ag_recv.at[b, slot],
            device_id=(peer, z),
            device_id_type=MESH,
        )

    def tgt_copies(k):
        index = f * n_t + k
        b, owner = index // n_f, index % n_f
        local = pltpu.make_async_copy(
            target_in.at[span(k)], tgt.at[b], tgt_recv.at[b]
        )
        remote = pltpu.make_async_remote_copy(
            src_ref=target_in.at[span(k)],
            dst_ref=tgt.at[b],
            send_sem=tgt_send.at[k],
            recv_sem=tgt_recv.at[b],
            device_id=(owner, z),
            device_id_type=MESH,
        )
        return owner, local, remote

    for c in range(n_c):
        hid_load(c).start()
        w_load(c).start()
        p_load(c).start()

    barrier = pltpu.get_barrier_semaphore()
    for d in range(1, n_f):
        pl.semaphore_signal(
            barrier, inc=1, device_id=((f + d) % n_f, z), device_id_type=MESH
        )

    @pl.when(z > 0)
    def _():
        pl.semaphore_signal(barrier, inc=1, device_id=(f, z - 1), device_id_type=MESH)

    @pl.when(z < n_t - 1)
    def _():
        pl.semaphore_signal(barrier, inc=1, device_id=(f, z + 1), device_id_type=MESH)

    near = jnp.where(z > 0, 1, 0) + jnp.where(z < n_t - 1, 1, 0)
    pl.semaphore_wait(barrier, n_f - 1 + near)

    @pl.when(z > 0)
    def _():
        for c in range(n_c):
            pass_on(hid_in, z, c, -1).start()

    @pl.when(z < n_t - 1)
    def _():
        for c in range(n_c):
            pass_on(hid_in, z, c, 1).start()

    for k in range(n_t):
        owner, local, remote = tgt_copies(k)
        pl.when(owner == f)(local.start)
        pl.when(owner != f)(remote.start)

    def finish(b):
        mine = part.at[b, span(f)]
        pltpu.make_async_copy(tgt.at[b], tgt.at[b], tgt_recv.at[b]).wait()
        for d in range(1, n_f):
            source = (f + n_f - d) % n_f
            rs_copy(b, source, source).wait_recv()
        total = mine[...].astype(jnp.float32)
        for d in range(1, n_f):
            total += rsbuf[b, (f + d) % n_f].astype(jnp.float32)
        stk[b, span(f)] = cotangents(total, tgt[b], cols, tokens)
        for d in range(1, n_f):
            ag_copy(b, (f + d) % n_f, f).start()

    for s in range(n_t):
        b = pick([order[i][s] for i in range(n_t)], z)

        def step(c, carry, s=s, b=b):
            if s == 0:
                hid_load(c).wait()
                w_load(c).wait()
                p_load(c).wait()
            else:
                pltpu.make_async_copy(
                    gath.at[b, cut(c)], gath.at[b, cut(c)], gath_recv.at[b, c]
                ).wait()

                @pl.when((b > z) & (z > 0))
                def _():
                    pass_on(gath.at[b], b, c, -1).start()

                @pl.when((b < z) & (z < n_t - 1))
                def _():
                    pass_on(gath.at[b], b, c, 1).start()

            for half in range(2):
                width = pl.ds(half * cols, cols)
                term = lax.dot_general(
                    gath[b, cut(c)],
                    wbuf[cut(c), width],
                    (((0,), (0,)), ((), ())),
                    preferred_element_type=jnp.float32,
                )
                acc[:, width] += term
            return carry

        acc[...] = jnp.zeros_like(acc)
        middle = n_c // 2
        lax.fori_loop(0, middle, step, 0)
        if s > 0:
            finish(pick([order[i][s - 1] for i in range(n_t)], z))
        lax.fori_loop(middle, n_c, step, 0)
        part[b] = acc[...].astype(jnp.bfloat16)
        for d in range(1, n_f):
            rs_copy(b, (f + d) % n_f, f).start()
    finish(pick([order[i][n_t - 1] for i in range(n_t)], z))

    def drain(b, carry):
        for d in range(1, n_f):
            source = (f + n_f - d) % n_f
            ag_copy(b, source, source).wait_recv()
            peer = (f + d) % n_f
            rs_copy(b, peer, f).wait_send()
            ag_copy(b, peer, f).wait_send()

        @pl.when((b >= z) & (z > 0))
        def _():
            for c in range(n_c):
                pass_on(hid_in, b, c, -1).wait_send()

        @pl.when((b <= z) & (z < n_t - 1))
        def _():
            for c in range(n_c):
                pass_on(hid_in, b, c, 1).wait_send()

        return carry

    lax.fori_loop(0, n_t, drain, 0)
    for k in range(n_t):
        owner, local, remote = tgt_copies(k)
        pl.when(owner != f)(remote.wait_send)


def moment_kernel(gath, stk, probe, grad_moment, curv_moment, new_grad, new_curv, update):
    n_t = gath.shape[0]
    hidden = jnp.concatenate([gath[b] for b in range(n_t)], axis=1)
    stacked = jnp.concatenate([stk[b] for b in range(n_t)], axis=0)
    products = jnp.dot(hidden, stacked, preferred_element_type=jnp.float32)
    new_grad[...], new_curv[...], update[...] = moments(
        products, probe[...], grad_moment[...], curv_moment[...]
    )


def kernel_shards(n_f, n_t, n_c, tile, hidden_t, down_weight, probe, grad_moment, curv_moment, target):
    rows, block_tokens = hidden_t.shape
    cols = down_weight.shape[1]
    piece = block_tokens // n_f
    bf16 = jnp.bfloat16
    dma = pltpu.SemaphoreType.DMA
    whole_vmem = pl.BlockSpec(memory_space=pltpu.VMEM)
    gath, stk = pl.pallas_call(
        functools.partial(cotangent_kernel, n_f, n_t, n_c),
        out_shape=(
            jax.ShapeDtypeStruct((n_t, rows, block_tokens), bf16),
            jax.ShapeDtypeStruct((n_t, block_tokens, 2 * cols), bf16),
        ),
        in_specs=[pl.BlockSpec(memory_space=pl.ANY)] * 4,
        out_specs=(whole_vmem, whole_vmem),
        scratch_shapes=[
            pltpu.VMEM((rows, 2 * cols), bf16),
            pltpu.VMEM((block_tokens, 2 * cols), jnp.float32),
            pltpu.VMEM((n_t, block_tokens, 2 * cols), bf16),
            pltpu.VMEM((n_t, n_f, piece, 2 * cols), bf16),
            pltpu.VMEM((n_t, piece, cols), bf16),
            dma((n_c,)), dma((n_c,)), dma((n_c,)),
            dma((n_t, n_c)), dma((n_t, n_c)), dma((n_t, n_c)),
            dma((n_t, n_f)), dma((n_t, n_f)), dma((n_t, n_f)), dma((n_t, n_f)),
            dma((n_t,)), dma((n_t,)),
        ],
        compiler_params=pltpu.CompilerParams(
            collective_id=0, has_side_effects=True, vmem_limit_bytes=44 * MIB
        ),
        name="cotangents",
    )(hidden_t, down_weight, probe, target)

    strip = pl.BlockSpec((tile, cols), lambda i: (i, 0))
    return pl.pallas_call(
        moment_kernel,
        grid=(rows // tile,),
        out_shape=(jax.ShapeDtypeStruct((rows, cols), bf16),) * 3,
        in_specs=[
            pl.BlockSpec((n_t, tile, block_tokens), lambda i: (0, i, 0)),
            pl.BlockSpec((n_t, block_tokens, 2 * cols), lambda i: (0, 0, 0)),
            strip, strip, strip,
        ],
        out_specs=(strip, strip, strip),
        compiler_params=pltpu.CompilerParams(vmem_limit_bytes=40 * MIB),
        name="moments",
    )(gath, stk, probe, grad_moment, curv_moment)


def solution(mesh):
    n_f, n_t = mesh.shape["fsdp"], mesh.shape["tensor"]

    def shards(hidden_t, down_weight, probe, grad_moment, curv_moment, target):
        rows, block_tokens = hidden_t.shape
        cols = down_weight.shape[1]
        n_c, tile = 7, 256
        fits = (
            n_f > 1 and n_t > 1
            and block_tokens % 128 == 0 and cols % 128 == 0
            and block_tokens % (16 * n_f) == 0
            and rows % (n_c * 128) == 0 and rows % tile == 0
        )
        args = (hidden_t, down_weight, probe, grad_moment, curv_moment, target)
        if not fits:
            return plain_shards(*args)
        return kernel_shards(n_f, n_t, n_c, tile, *args)

    spec = P("fsdp", "tensor")
    return jax.shard_map(
        shards, mesh=mesh, in_specs=(spec,) * 6, out_specs=(spec,) * 3, check_vma=False
    )
```
